128 devices in a mesh: exp: 64 (over z, y, x), grp: 2 (over core).
Axes of the slice: x: 4, y: 4, z: 4, core: 2. Of those that a mesh axis runs over, the one named last changes fastest.
Arguments:
- tokens: bfloat16 [65536, 3584], P(('exp', 'grp')), may hold values from -6 to 6
- routes: int32 [65536, 1], P(('exp', 'grp')), may hold values from 0 to 63; in each aligned block of 512 rows (0 to 511, 512 to 1023, ...) at most 12 rows name the same one
- gate_prob: float32 [65536, 1], P(('exp', 'grp')), may hold values from 0.1 to 1
- w_gate: bfloat16 [64, 3584, 1024], P('exp', None, 'grp'), may hold values from -0.09375 to 0.09375
- w_up: bfloat16 [64, 3584, 1024], P('exp', None, 'grp'), may hold values from -0.09375 to 0.09375
- hidden_grad: bfloat16 [64, 1536, 1024], P('exp', None, 'grp'), may hold values from -0.1875 to 0.1875
Outputs:
- grad_gate: bfloat16 [64, 3584, 1024], P('exp', None, 'grp')
- grad_up: bfloat16 [64, 3584, 1024], P('exp', None, 'grp')
- prob_grad: float32 [65536, 1], P(('exp', 'grp'))
The draws below stay inside these ranges and needn't reach their ends.
Inputs may be any that keep to these rules, and one draw needn't show every extreme that they name: Among the 512 tokens of one device at most 12 routes go to any one expert, and in every draw some device sends exactly 12 to some expert.
All inputs are finite; a program needn't handle non-finite values.
Results may differ from the reference program's by a relative error of at most 0.0056.
Values may be sent and summed in bfloat16 or wider, within the bound.
A program may use at most 128 MiB of HBM per device.

```python
import math
import jax
import jax.numpy as jnp
import numpy as np
from jax import lax

D = 3584
FF = 1024
TOK_DEV = 512
TOP = 1
EXPERTS = 64
CAP = 12
SLOTS = 1536
TOKENS = 65536
N_EXP = 64
N_GRP = 2


def levels(stream_key, shape, shards, least, top_value):
    def one(dim, shards_of):
        steps = jax.random.uniform(jax.random.fold_in(jax.random.fold_in(stream_key, 6), dim), (shards_of,), jnp.float32, least / len(shards), top_value / len(shards))
        return jnp.repeat(jnp.exp(steps), shape[dim] // shards_of).reshape((-1,) + (1,) * (len(shape) - dim - 1))

    level = one(*shards[0])
    for cut in shards[1:]:
        level = level * one(*cut)
    return level


def deal_out(stream_key, own, number, rows, amount, top, most, lean):
    sequence = jax.random.permutation(stream_key, amount)
    heavy_load, ordinary = portions_of(amount, rows * top, most, lean, True), portions_of(amount, rows * top, most, lean, False)
    places = jnp.arange(amount)

    def named(sizes, rotation):
        used = int((sizes > 0).sum())
        fixed = max(1, used // 4)
        moved = fixed + (places - fixed + rotation * (used - fixed)) % max(1, amount - fixed)
        return jnp.zeros((amount,), jnp.int32).at[sequence[jnp.where(places < fixed, places, moved)]].set(jnp.asarray(sizes, jnp.int32))

    sizes = jnp.where(number % 4 == 0, named(heavy_load, number // 4), named(ordinary, number - number // 4 - 1))
    mixed = jax.random.permutation(jax.random.fold_in(own, 3), amount)
    giver, sink = mixed[0:amount // 2 * 2:2], mixed[1:amount // 2 * 2:2]
    margin = jnp.minimum(sizes[giver] - 1, most - sizes[sink]) // 2
    margin = jnp.where((giver == sequence[0]) | (sink == sequence[0]) | (sizes[sink] == 0), 0, jnp.maximum(margin, 0))
    moved = jax.random.randint(jax.random.fold_in(own, 4), (amount // 2,), 0, 1 << 20) % (margin + 1)
    sizes = sizes.at[giver].add(-moved).at[sink].add(moved)
    items = jnp.searchsorted(jnp.cumsum(sizes), jnp.arange(rows * top), side="right").astype(jnp.int32)
    grid = items.reshape(top, rows).T
    grid = grid[jax.random.permutation(jax.random.fold_in(own, 1), rows)]
    rotation = jax.random.randint(jax.random.fold_in(own, 2), (rows, 1), 0, top)
    return jnp.take_along_axis(grid, (jnp.arange(top)[None, :] + rotation) % top, axis=1)


def portions_of(count, total, reach, lean, full):
    portions = [(1 << 20) // math.isqrt(standing ** lean) + 1 for standing in range(1, count + 1)]
    largest = reach if full else min(reach, max(-(-total // count), total * portions[0] // sum(portions)))
    least = 1 if total - largest >= count - 1 else 0
    holding, rest = [largest] + [least] * (count - 1), total - largest - least * (count - 1)
    while rest > 0:
        free = [i for i in range(1, count) if holding[i] < largest] or [i for i in range(1, count) if holding[i] < reach]
        whole, budget = sum([portions[i] for i in free]), rest
        for i in free:
            extra = min(reach - holding[i], max(1, budget * portions[i] // whole), rest)
            holding[i] = holding[i] + extra
            rest = rest - extra
    return np.array(holding)


def bell_draw(key, dims, spread, most, pieces=(), held_as=jnp.bfloat16):
    level = levels(key, dims, pieces, -0.22, 0.18) if pieces else 1.0
    values = jax.random.normal(key, dims, jnp.float32) * spread * level
    return jnp.minimum(jnp.maximum(values, -most), most).astype(held_as)


def setup_inputs(seed: int = 0) -> dict:
    arg_keys = jax.random.split(jax.random.key(seed), 7)
    tokens = bell_draw(arg_keys[0], (TOKENS, D), 1.0, 6.0, ((0, 128),))
    routes_keys = jax.random.split(jax.random.fold_in(arg_keys[1], 1), TOKENS // TOK_DEV)
    routes_turns = jax.random.permutation(jax.random.fold_in(arg_keys[1], 3), TOKENS // TOK_DEV)
    routes = jax.vmap(lambda own, number: deal_out(jax.random.fold_in(arg_keys[1], 2), own, number, TOK_DEV, EXPERTS, TOP, CAP, 2))(routes_keys, routes_turns).reshape((TOKENS, TOP))
    gate_prob = jnp.clip(jnp.exp(math.log(1.0) - 2.3025851 * jax.random.uniform(arg_keys[2], (TOKENS, TOP), jnp.float32) ** levels(arg_keys[2], (TOKENS, TOP), ((0, 128),), -0.2, 0.2)), 0.1, 1.0)
    w_gate = bell_draw(arg_keys[3], (EXPERTS, D, FF), D ** -0.5, 0.09375, ((0, 64), (2, 2)))
    w_up = bell_draw(arg_keys[4], (EXPERTS, D, FF), D ** -0.5, 0.09375, ((0, 64), (2, 2)))
    hidden_grad = bell_draw(arg_keys[5], (EXPERTS, SLOTS, FF), 0.03, 0.1875, ((0, 64), (2, 2)))
    return dict(tokens=tokens, routes=routes, gate_prob=gate_prob, w_gate=w_gate, w_up=w_up, hidden_grad=hidden_grad)


def reference(tokens, routes, gate_prob, w_gate, w_up, hidden_grad):
    blocks = N_EXP * N_GRP
    per_block = TOK_DEV * TOP
    flat_ids = routes.reshape(blocks, per_block).astype(jnp.int32)
    expert_list = jnp.arange(EXPERTS, dtype=jnp.int32)
    member = (flat_ids[:, :, None] == expert_list[None, None, :]).astype(jnp.int32)
    earlier = jnp.cumsum(member, axis=1) - member
    position = jnp.sum(earlier * member, axis=2).astype(jnp.int32)
    block_ids = jnp.arange(blocks, dtype=jnp.int32)
    source_exp = block_ids // N_GRP
    source_grp = block_ids % N_GRP
    slot_index = source_grp[:, None] * (N_EXP * CAP) + source_exp[:, None] * CAP + position
    target = (flat_ids * SLOTS + slot_index).reshape(-1).astype(jnp.int32)
    route_rows = jnp.repeat(tokens, TOP, axis=0)
    expert_rows = jnp.zeros((EXPERTS * SLOTS, D), jnp.bfloat16).at[target].set(route_rows).reshape(EXPERTS, SLOTS, D)
    slot_prob = jnp.zeros((EXPERTS * SLOTS,), jnp.bfloat16).at[target].set(gate_prob.reshape(-1).astype(jnp.bfloat16))
    slot_prob = slot_prob.reshape(EXPERTS, SLOTS)

    def per_expert(items):
        rows, probs, weight_gate, weight_up, cotangent = items
        gate_proj = jnp.dot(rows, weight_gate, preferred_element_type=jnp.float32)
        up_proj = jnp.dot(rows, weight_up, preferred_element_type=jnp.float32)
        sigmoid_gate = jax.nn.sigmoid(gate_proj)
        activated = gate_proj * sigmoid_gate
        cot_values = cotangent.astype(jnp.float32)
        slot_grad = jnp.sum(activated * up_proj * cot_values, axis=1)
        scaled = probs.astype(jnp.float32)[:, None] * cot_values
        up_term = (scaled * activated).astype(jnp.bfloat16)
        gate_term = (scaled * up_proj * sigmoid_gate * (1.0 + gate_proj * (1.0 - sigmoid_gate))).astype(jnp.bfloat16)
        grad_g = jnp.dot(rows.T, gate_term, preferred_element_type=jnp.float32).astype(jnp.bfloat16)
        grad_u = jnp.dot(rows.T, up_term, preferred_element_type=jnp.float32).astype(jnp.bfloat16)
        return grad_g, grad_u, slot_grad

    grad_gate, grad_up, slot_grad = lax.map(per_expert, (expert_rows, slot_prob, w_gate, w_up, hidden_grad))
    prob_grad = slot_grad.reshape(-1)[target].reshape(TOKENS, TOP)
    return grad_gate, grad_up, prob_grad
```

```python
import jax
import jax.numpy as jnp
from jax import lax
from jax.experimental import pallas as pl
from jax.experimental.pallas import tpu as pltpu
from jax.sharding import PartitionSpec as P

BF16, F32, I32 = jnp.bfloat16, jnp.float32, jnp.int32
MESH = pl.DeviceIdType.MESH
HIGH = lax.Precision.HIGHEST

D = 3584
HALF = 512
TOK = 512
N_EXP = 64
CAP = 12
PART = 896
MAIN = 3 * PART
STEPS = 8
ROWS = 192
GROUP = 48
TILE = 512
CHUNKS = ((0, 8), (8, 24), (32, 32))


def kernel(
    tok_hbm, routes_ref, prob_ref, wg_hbm, wu_hbm, hg_hbm,
    gg_hbm, gu_hbm, pg_ref,
    tok, send, recv, rows, wg, wu, hg, acc, terms, stage, member_ref,
    prs, pr_own, pr_part, ret_out, ret_own, ret_part,
    send_sem, recv_sem, prs_sem, prr_sem, rets_sem, retr_sem,
    fwds_sem, fwdr_sem, part_sem, load_sem, out_sem, self_sem,
):
    me = lax.axis_index("exp")
    g = lax.axis_index("grp")
    z, y, x = me // 16, (me // 4) % 4, me % 4
    partner = {"exp": me, "grp": 1 - g}

    def target(k, m, dx):
        dz, dy = k // 4 + 2 * m, k % 4 + 2 * m
        return ((z + dz) % 4) * 16 + ((y + dy) % 4) * 4 + (x + dx) % 4

    def group_of(k, m):
        dz, dy = k // 4 + 2 * m, k % 4 + 2 * m
        return ((z + 8 - dz) % 4) * 4 + (y + 8 - dy) % 4

    barrier = pltpu.get_barrier_semaphore()

    @pl.loop(1, N_EXP)
    def _(i):
        pl.semaphore_signal(barrier, inc=1, device_id={"exp": (me + i) % N_EXP, "grp": g}, device_id_type=MESH)

    pl.semaphore_signal(barrier, inc=1, device_id=partner, device_id_type=MESH)

    def columns(p):
        return pl.ds(p * PART, PART)

    tok_loads = [pltpu.make_async_copy(tok_hbm.at[:, columns(p)], tok.at[:, columns(p)], load_sem.at[p]) for p in range(4)]
    for p in (3, 0, 1, 2):
        tok_loads[p].start()
    w_loads = [
        pltpu.make_async_copy(wg_hbm.at[0], wg, load_sem.at[4]),
        pltpu.make_async_copy(wu_hbm.at[0], wu, load_sem.at[5]),
        pltpu.make_async_copy(hg_hbm.at[0], hg, load_sem.at[6]),
    ]
    for load in w_loads:
        load.start()

    r = lax.broadcasted_iota(I32, (N_EXP, TOK), 0)
    rk, rm, rx = r >> 3, (r >> 2) & 1, r & 3
    expert = ((z + (rk >> 2) + 2 * rm) & 3) * 16 + ((y + (rk & 3) + 2 * rm) & 3) * 4 + ((x + rx) & 3)
    member = jnp.where(expert == routes_ref[...], 1.0, 0.0).astype(F32)
    member_ref[...] = member
    before = lax.broadcasted_iota(I32, (TOK, TOK), 0) < lax.broadcasted_iota(I32, (TOK, TOK), 1)
    earlier = jnp.dot(member.astype(BF16), jnp.where(before, 1.0, 0.0).astype(BF16), preferred_element_type=F32)
    pos = jnp.sum(member * earlier, axis=0, keepdims=True).astype(I32)
    rank = jnp.sum(member * r.astype(F32), axis=0, keepdims=True).astype(I32)
    main_row = rank * 16 + ((12 * x + pos) & 15)
    tail_row = rank * 8 + (pos & 3)
    tail_part = pos >> 2
    tail_first = (12 * x + 12) % 16
    i16 = lax.broadcasted_iota(I32, (1, 16, PART), 1)
    tail_mask = (i16 >= tail_first) & (i16 < tail_first + 4)

    lane_slot = lax.broadcasted_iota(I32, (128, TOK), 0)
    prob_at = jnp.where(lane_slot == pos, prob_ref[...], 0.0).astype(BF16)
    prs[:, 0, :] = lax.dot_general(member.astype(BF16), prob_at, (((1,), (1,)), ((), ())), preferred_element_type=F32)

    def send_copy(k, m, dx):
        rk_ = k * 8 + m * 4 + dx
        slot = (k * 2 + m) * 4 + x
        return pltpu.make_async_remote_copy(
            send.at[rk_], recv.at[slot], send_sem.at[rk_], recv_sem.at[slot],
            device_id={"exp": target(k, m, dx), "grp": g}, device_id_type=MESH)

    def prob_copy(k, m, dx):
        rk_ = k * 8 + m * 4 + dx
        slot = (k * 2 + m) * 4 + x
        return pltpu.make_async_remote_copy(
            prs.at[rk_], pr_own.at[slot], prs_sem.at[rk_], prr_sem.at[slot],
            device_id={"exp": target(k, m, dx), "grp": g}, device_id_type=MESH)

    def return_copy(k, m, sx):
        idx = k * 8 + m * 4 + sx
        slot = k * 8 + m * 4 + (x + 4 - sx) % 4
        return pltpu.make_async_remote_copy(
            ret_out.at[idx], ret_own.at[slot], rets_sem.at[idx], retr_sem.at[slot],
            device_id={"exp": group_of(k, m) * 4 + sx, "grp": g}, device_id_type=MESH)

    self_rows = pltpu.make_async_copy(send.at[0], recv.at[x], self_sem.at[0])
    self_prob = pltpu.make_async_copy(prs.at[0], pr_own.at[x], self_sem.at[1])
    self_ret = pltpu.make_async_copy(ret_out.at[x], ret_own.at[0], self_sem.at[2])

    def build(first, count):
        hit = lax.broadcasted_iota(I32, (16 * count, TOK), 0) + 16 * first == main_row
        pick = jnp.where(hit, 1.0, 0.0).astype(BF16)
        it = lax.broadcasted_iota(I32, (8 * count, TOK), 0) + 8 * first
        picks = []
        for p in range(3):
            own = jnp.where(tail_part == p, tail_row, -100)
            picks.append(jnp.where((it == own) | (it == own + 4), 1.0, 0.0).astype(BF16))
        if first == 0:
            tok_loads[3].wait()
        tails = jnp.dot(jnp.concatenate(picks, axis=0), tok[:, MAIN:], preferred_element_type=F32)
        for p in range(3):
            if first == 0:
                tok_loads[p].wait()
            main = jnp.dot(pick, tok[:, p * PART:(p + 1) * PART], preferred_element_type=F32)
            tail = tails[p * 8 * count:(p + 1) * 8 * count].reshape(count, 8, PART)
            both = jnp.concatenate([tail, tail], axis=1)
            block = jnp.where(tail_mask, both, main.reshape(count, 16, PART)).astype(BF16)
            send[first:first + count, :, p * PART:(p + 1) * PART] = block

    for first, count in CHUNKS:
        build(first, count)
        if first == 0:
            pl.semaphore_wait(barrier, N_EXP)
            self_rows.start()
            self_prob.start()

        @pl.loop(max(first, 1), first + count)
        def _(i):
            m = i % 2
            send_copy(i // 8, m, ((i % 8) // 2 + 2 * m) % 4).start()

        if first == 0:
            @pl.loop(1, N_EXP)
            def _(i):
                prob_copy(i // 8, (i // 4) % 2, i % 4).start()

    acc[...] = jnp.zeros_like(acc)

    @pl.loop(1, N_EXP)
    def _(i):
        k, m, dx = i // 8, (i // 4) % 2, i % 4
        slot = (k * 2 + m) * 4 + (x + 4 - dx) % 4
        pltpu.make_async_remote_copy(
            prs.at[0], pr_own.at[slot], prs_sem.at[0], prr_sem.at[slot], device_id=partner, device_id_type=MESH).wait_recv()

    self_prob.wait()
    prob_forward = pltpu.make_async_remote_copy(
        pr_own, pr_part, part_sem.at[0], part_sem.at[1], device_id=partner, device_id_type=MESH)
    prob_forward.start()
    prob_forward.wait_recv()
    for load in w_loads:
        load.wait()

    def forward_copy(k):
        return pltpu.make_async_remote_copy(
            rows.at[k, g], rows.at[k, g], fwds_sem.at[k], fwdr_sem.at[k], device_id=partner, device_id_type=MESH)

    low = lax.broadcasted_iota(I32, (8, PART), 0) < 4

    def unpack(k, m):
        base = (k * 2 + m) * 4

        def half(s, h, p):
            return recv[base + s, :, p * PART:(p + 1) * PART].astype(F32)[8 * h:8 * h + 8]

        def put(t, p, lo, hi):
            rows[k, g, m * GROUP + 16 * t:m * GROUP + 16 * t + 16, p * PART:(p + 1) * PART] = jnp.concatenate(
                [lo, hi], axis=0).astype(BF16)

        for p in range(3):
            put(0, p, half(0, 0, p), jnp.where(low, half(0, 1, p), half(1, 1, p)))
            put(1, p, half(1, 0, p), half(2, 1, p))
            put(2, p, jnp.where(low, half(2, 0, p), half(3, 0, p)), half(3, 1, p))

        def quad(q):
            s, p = q // 3, q % 3
            at = 3 - s
            value = half(s, at // 2, p)
            return value if at % 2 == q % 2 else pltpu.roll(value, 4, 0)

        for t in range(3):
            lo, hi = (jnp.where(low, quad(4 * t + 2 * h), quad(4 * t + 2 * h + 1)) for h in range(2))
            put(t, 3, lo, hi)

    row16 = lax.broadcasted_iota(I32, (ROWS, 16), 0)
    at16 = lax.broadcasted_iota(I32, (ROWS, 16), 1) * CAP
    spread = jnp.where((row16 >= at16) & (row16 < at16 + CAP), 1.0, 0.0)
    row_t = lax.broadcasted_iota(I32, (16, ROWS), 1)
    at_t = lax.broadcasted_iota(I32, (16, ROWS), 0) * CAP
    spread_t = jnp.where((row_t >= at_t) & (row_t < at_t + CAP), 1.0, 0.0)
    row128 = lax.broadcasted_iota(I32, (ROWS, 128), 0)
    lane_hit = lax.broadcasted_iota(I32, (ROWS, 128), 1) == row128 - ((row128 * 5462) >> 16) * CAP

    def step(k):
        for m in range(2):
            for s in range(4):
                slot = (k * 2 + m) * 4 + s
                wait = pltpu.make_async_remote_copy(
                    send.at[0], recv.at[slot], send_sem.at[0], recv_sem.at[slot], device_id=partner, device_id_type=MESH)
                if m == 0:
                    own = (k == 0) & (x == s)
                    pl.when(own)(self_rows.wait)
                    pl.when(jnp.logical_not(own))(wait.wait_recv)
                else:
                    wait.wait_recv()
        unpack(k, 0)
        unpack(k, 1)
        forward = forward_copy(k)
        forward.start()
        own_p, other_p = pr_own[pl.ds(k * 8, 8), 0, :], pr_part[pl.ds(k * 8, 8), 0, :]
        first = g == 0
        probs = jnp.concatenate([jnp.where(first, own_p, other_p), jnp.where(first, other_p, own_p)], axis=0)
        probs = jnp.dot(spread.astype(BF16), probs.astype(BF16), preferred_element_type=F32)
        prob = jnp.sum(jnp.where(lane_hit, probs, 0.0), axis=1, keepdims=True)
        forward.wait_recv()
        total = jnp.zeros((ROWS, 1), F32)
        width = 256
        for n in range(HALF // width):
            sl = slice(n * width, (n + 1) * width)
            here = rows[k].reshape(ROWS, D)
            gate = jnp.dot(here, wg[:, sl], preferred_element_type=F32)
            up = jnp.dot(here, wu[:, sl], preferred_element_type=F32)
            pieces = [
                hg[pl.ds(pl.multiple_of(j * 768 + group_of(k, m) * GROUP, 16), GROUP), sl] for j in range(2) for m in range(2)]
            cot = jnp.concatenate(pieces, axis=0).astype(F32)
            sig = jax.nn.sigmoid(gate)
            act = gate * sig
            total = total + jnp.sum(act * up * cot, axis=1, keepdims=True)
            scaled = prob * cot
            terms[k, :, sl] = (scaled * up * sig * (1.0 + gate * (1.0 - sig))).astype(BF16)
            terms[k, :, HALF + n * width:HALF + (n + 1) * width] = (scaled * act).astype(BF16)
        by_source = jnp.dot(
            spread_t, jnp.where(lane_hit, total, 0.0), precision=HIGH, preferred_element_type=F32)
        ret_out[pl.ds(k * 8, 8), 0, :] = by_source[0:8]
        ret_out[pl.ds(k * 8, 8), 1, :] = by_source[8:16]
        for m in range(2):
            for s in range(4):
                copy = return_copy(k, m, s)
                if m == 0:
                    own = (k == 0) & (x == s)
                    pl.when(own)(self_ret.start)
                    pl.when(jnp.logical_not(own))(copy.start)
                else:
                    copy.start()

    def product(k, count, sl):
        left = rows[pl.ds(k, count), :, :, sl].reshape(count * ROWS, TILE)
        right = terms[pl.ds(k, count)].reshape(count * ROWS, 2 * HALF)
        return lax.dot_general(left, right, (((0,), (0,)), ((), ())), preferred_element_type=F32)

    def tile(i):
        return pl.ds(pl.multiple_of(i * TILE, TILE), TILE)

    def accumulate(k, count):
        @pl.loop(0, D // TILE)
        def _(i):
            acc[tile(i), :] += product(k, count, tile(i))

    @pl.loop(0, STEPS)
    def _(k):
        step(k)

        @pl.when((k == 1) | (k == 3) | (k == 5))
        def _():
            accumulate(k - 1, 2)

        @pl.when(k == 6)
        def _():
            accumulate(6, 1)

    def out_copies(i, b):
        return (
            pltpu.make_async_copy(stage.at[b, :, pl.ds(0, HALF)], gg_hbm.at[0, tile(i), :], out_sem.at[b, 0]),
            pltpu.make_async_copy(stage.at[b, :, pl.ds(HALF, HALF)], gu_hbm.at[0, tile(i), :], out_sem.at[b, 1]),
        )

    @pl.loop(0, D // TILE)
    def _(i):
        b = i % 2

        @pl.when(i >= 2)
        def _():
            for copy in out_copies(i - 2, b):
                copy.wait()

        stage[b] = (acc[tile(i), :] + product(STEPS - 1, 1, tile(i))).astype(BF16)
        for copy in out_copies(i, b):
            copy.start()

    @pl.loop(1, N_EXP)
    def _(i):
        pltpu.make_async_remote_copy(
            ret_out.at[0], ret_own.at[i], rets_sem.at[0], retr_sem.at[i], device_id=partner, device_id_type=MESH).wait_recv()

    self_ret.wait()
    ret_forward = pltpu.make_async_remote_copy(
        ret_own, ret_part, part_sem.at[2], part_sem.at[3], device_id=partner, device_id_type=MESH)
    ret_forward.start()
    ret_forward.wait_recv()
    sums = jnp.where(g == 0, ret_own[:, 0, :] + ret_part[:, 0, :], ret_own[:, 1, :] + ret_part[:, 1, :])
    by_slot = lax.dot_general(
        sums, member_ref[...], (((0,), (0,)), ((), ())), precision=HIGH, preferred_element_type=F32)
    pg_ref[...] = jnp.sum(jnp.where(lane_slot == pos, by_slot, 0.0), axis=0, keepdims=True)

    for i in (D // TILE - 2, D // TILE - 1):
        for copy in out_copies(i, i % 2):
            copy.wait()
    prob_forward.wait_send()
    ret_forward.wait_send()

    @pl.loop(1, N_EXP)
    def _(i):
        k, m, dx = i // 8, (i // 4) % 2, i % 4
        send_copy(k, m, dx).wait_send()
        prob_copy(k, m, dx).wait_send()

    @pl.loop(0, N_EXP)
    def _(i):
        k, m, s = i // 8, (i // 4) % 2, i % 4

        @pl.when((i >= 4) | (s != x))
        def _():
            return_copy(k, m, s).wait_send()

    @pl.loop(0, STEPS)
    def _(k):
        forward_copy(k).wait_send()


def body(tokens, routes, gate_prob, w_gate, w_up, hidden_grad):
    hbm = pl.BlockSpec(memory_space=pl.ANY)
    vmem = pl.BlockSpec(memory_space=pltpu.VMEM)
    dma = pltpu.SemaphoreType.DMA
    grad = jax.ShapeDtypeStruct((1, D, HALF), BF16)
    grad_gate, grad_up, prob_grad = pl.pallas_call(
        kernel,
        out_shape=(grad, grad, jax.ShapeDtypeStruct((1, TOK), F32)),
        in_specs=[hbm, vmem, vmem, hbm, hbm, hbm],
        out_specs=(hbm, hbm, vmem),
        scratch_shapes=[
            pltpu.VMEM((TOK, D), BF16),
            pltpu.VMEM((N_EXP, 16, MAIN), BF16),
            pltpu.VMEM((N_EXP, 16, MAIN), BF16),
            pltpu.VMEM((STEPS, 2, 2 * GROUP, D), BF16),
            pltpu.VMEM((D, HALF), BF16),
            pltpu.VMEM((D, HALF), BF16),
            pltpu.VMEM((1536, HALF), BF16),
            pltpu.VMEM((D, 2 * HALF), F32),
            pltpu.VMEM((STEPS, ROWS, 2 * HALF), BF16),
            pltpu.VMEM((2, TILE, 2 * HALF), BF16),
            pltpu.VMEM((N_EXP, TOK), F32),
            pltpu.VMEM((N_EXP, 1, 128), F32),
            pltpu.VMEM((N_EXP, 1, 128), F32),
            pltpu.VMEM((N_EXP, 1, 128), F32),
            pltpu.VMEM((N_EXP, 2, 128), F32),
            pltpu.VMEM((N_EXP, 2, 128), F32),
            pltpu.VMEM((N_EXP, 2, 128), F32),
            dma((N_EXP,)), dma((N_EXP,)), dma((N_EXP,)), dma((N_EXP,)), dma((N_EXP,)), dma((N_EXP,)),
            dma((STEPS,)), dma((STEPS,)), dma((4,)), dma((7,)), dma((2, 2)), dma((3,)),
        ],
        compiler_params=pltpu.CompilerParams(
            collective_id=0, has_side_effects=True, vmem_limit_bytes=63 * 1024 * 1024),
        cost_estimate=pl.CostEstimate(flops=26 * 10**9, bytes_accessed=20 * 10**6, transcendentals=10**6),
        name="moe_grads",
    )(tokens, routes.reshape(1, TOK), gate_prob.reshape(1, TOK), w_gate, w_up, hidden_grad)
    return grad_gate, grad_up, prob_grad.reshape(TOK, 1)


def solution(mesh):
    in_specs = (
        P(("exp", "grp"), None),
        P(("exp", "grp"), None),
        P(("exp", "grp"), None),
        P("exp", None, "grp"),
        P("exp", None, "grp"),
        P("exp", None, "grp"),
    )
    out_specs = (P("exp", None, "grp"), P("exp", None, "grp"), P(("exp", "grp"), None))
    return jax.shard_map(body, mesh=mesh, in_specs=in_specs, out_specs=out_specs, check_vma=False)
```

```python
import jax
import jax.numpy as jnp
from jax import lax
from jax.experimental import pallas as pl
from jax.experimental.pallas import tpu as pltpu
from jax.sharding import PartitionSpec as P

BF16, F32, I32 = jnp.bfloat16, jnp.float32, jnp.int32
MESH = pl.DeviceIdType.MESH
HIGH = lax.Precision.HIGHEST

D = 3584
HALF = 512
TOK = 512
N_EXP = 64
CAP = 12
PART = 896
MAIN = 3 * PART
STEPS = 8
ROWS = 192
GROUP = 48
TILE = 896
AHEAD = 3
CHUNKS = ((0, 8), (8, 16), (24, 40))


def kernel(
    tok_hbm, routes_ref, prob_ref, wg_hbm, wu_hbm, hg_hbm,
    gg_ref, gu_ref, pg_ref,
    tok, send, recv, rows, wg, wu, hg, terms, member_ref,
    prs, pr_own, pr_part, ret_out, ret_own,
    send_sem, recv_sem, prs_sem, prr_sem, rets_sem, retr_sem,
    fwds_sem, fwdr_sem, pfs_sem, pfr_sem, load_sem, self_sem,
):
    me = lax.axis_index("exp")
    g = lax.axis_index("grp")
    z, y, x = lax.div(me, 16), lax.rem(lax.div(me, 4), 4), lax.rem(me, 4)
    partner = {"exp": me, "grp": 1 - g}
    zs = [lax.rem(z + d, 4) * 16 for d in range(4)]
    ys = [lax.rem(y + d, 4) * 4 for d in range(4)]
    xs = [lax.rem(x + d, 4) for d in range(4)]

    def target(k, m, dx):
        return zs[(k // 4 + 2 * m) % 4] + ys[(k % 4 + 2 * m) % 4] + xs[dx]

    def send_step(k):
        slot, group = [], []
        for m in range(2):
            dz, dy = lax.div(k, 4) + 2 * m, lax.rem(k, 4) + 2 * m
            group.append(lax.rem(z + dz, 4) * 16 + lax.rem(y + dy, 4) * 4)
            slot.append((k * 2 + m) * 4 + x)
        for i in range(8):
            m = i % 2
            dx = (i // 2 + 2 * m) % 4
            pltpu.make_async_remote_copy(
                send.at[k * 8 + m * 4 + dx], recv.at[slot[m]], send_sem, recv_sem.at[k * 2 + m],
                device_id={"exp": group[m] + xs[dx], "grp": g}, device_id_type=MESH).start()
            pltpu.make_async_remote_copy(
                prs.at[k * 8 + m * 4 + dx], pr_own.at[slot[m]], prs_sem, prr_sem.at[k],
                device_id={"exp": group[m] + xs[dx], "grp": g}, device_id_type=MESH).start()

    def group_of(k, m):
        dz, dy = lax.div(k, 4) + 2 * m, lax.rem(k, 4) + 2 * m
        return lax.rem(z + 8 - dz, 4) * 4 + lax.rem(y + 8 - dy, 4)

    def columns(p):
        return pl.ds(p * PART, PART)

    tok_loads = [pltpu.make_async_copy(tok_hbm.at[:, columns(p)], tok.at[:, columns(p)], load_sem.at[p]) for p in range(4)]
    for p in (3, 0, 1, 2):
        tok_loads[p].start()
    barrier = pltpu.get_barrier_semaphore()
    for i in range(1, N_EXP):
        pl.semaphore_signal(
            barrier, inc=1, device_id={"exp": target(i // 8, (i // 4) % 2, i % 4), "grp": g}, device_id_type=MESH)

    pl.semaphore_signal(barrier, inc=1, device_id=partner, device_id_type=MESH)

    w_loads = [
        pltpu.make_async_copy(wg_hbm.at[0], wg, load_sem.at[4]),
        pltpu.make_async_copy(wu_hbm.at[0], wu, load_sem.at[5]),
        pltpu.make_async_copy(hg_hbm.at[0], hg, load_sem.at[6]),
    ]
    for load in w_loads:
        load.start()

    r = lax.broadcasted_iota(I32, (N_EXP, TOK), 0)
    rk, rm, rx = r >> 3, (r >> 2) & 1, r & 3
    expert = ((z + (rk >> 2) + 2 * rm) & 3) * 16 + ((y + (rk & 3) + 2 * rm) & 3) * 4 + ((x + rx) & 3)
    member = jnp.where(expert == routes_ref[...], 1.0, 0.0).astype(F32)
    member_ref[...] = member
    before = lax.broadcasted_iota(I32, (TOK, TOK), 0) < lax.broadcasted_iota(I32, (TOK, TOK), 1)
    earlier = jnp.dot(member.astype(BF16), jnp.where(before, 1.0, 0.0).astype(BF16), preferred_element_type=F32)
    pos = jnp.sum(member * earlier, axis=0, keepdims=True).astype(I32)
    rank = jnp.sum(member * r.astype(F32), axis=0, keepdims=True).astype(I32)
    main_row = rank * 16 + ((12 * x + pos) & 15)
    tail_row = rank * 8 + (pos & 3)
    tail_part = pos >> 2
    tail_first = (12 * x + 12) % 16
    i16 = lax.broadcasted_iota(I32, (1, 16, PART), 1)
    tail_mask = (i16 >= tail_first) & (i16 < tail_first + 4)

    lane_slot = lax.broadcasted_iota(I32, (128, TOK), 0)
    prob_at = jnp.where(lane_slot == pos, prob_ref[...], 0.0).astype(BF16)
    prs[:, 0, :] = lax.dot_general(member.astype(BF16), prob_at, (((1,), (1,)), ((), ())), preferred_element_type=F32)

    def send_copy(k, m, dx):
        rk_ = k * 8 + m * 4 + dx
        slot = (k * 2 + m) * 4 + x
        return pltpu.make_async_remote_copy(
            send.at[rk_], recv.at[slot], send_sem, recv_sem.at[k * 2 + m],
            device_id={"exp": target(k, m, dx), "grp": g}, device_id_type=MESH)

    def prob_copy(k, m, dx):
        rk_ = k * 8 + m * 4 + dx
        slot = (k * 2 + m) * 4 + x
        return pltpu.make_async_remote_copy(
            prs.at[rk_], pr_own.at[slot], prs_sem, prr_sem.at[k],
            device_id={"exp": target(k, m, dx), "grp": g}, device_id_type=MESH)

    def return_copy(k, m, sx, group, j):
        slot = g * N_EXP + k * 8 + m * 4 + xs[(4 - sx) % 4]
        return pltpu.make_async_remote_copy(
            ret_out.at[j * N_EXP + k * 8 + m * 4 + sx], ret_own.at[slot], rets_sem, retr_sem,
            device_id={"exp": group * 4 + sx, "grp": j}, device_id_type=MESH)

    def peers_copy(source, landing, first, out_sem_, in_sem_, count=N_EXP - 1):
        return pltpu.make_async_remote_copy(
            source.at[pl.ds(first, count)], landing.at[pl.ds(first, count)], out_sem_, in_sem_,
            device_id=partner, device_id_type=MESH)

    self_rows = pltpu.make_async_copy(send.at[0], recv.at[x], self_sem.at[0])
    self_prob = pltpu.make_async_copy(prs.at[0], pr_own.at[x], self_sem.at[1])
    self_ret = pltpu.make_async_copy(ret_out.at[g * N_EXP + x], ret_own.at[g * N_EXP], self_sem.at[2])

    def build(first, count):
        hit = lax.broadcasted_iota(I32, (16 * count, TOK), 0) + 16 * first == main_row
        pick = jnp.where(hit, 1.0, 0.0).astype(BF16)
        it = lax.broadcasted_iota(I32, (8 * count, TOK), 0) + 8 * first
        picks = []
        for p in range(3):
            own = jnp.where(tail_part == p, tail_row, -100)
            picks.append(jnp.where((it == own) | (it == own + 4), 1.0, 0.0).astype(BF16))
        if first == 0:
            tok_loads[3].wait()
        tails = jnp.dot(jnp.concatenate(picks, axis=0), tok[:, MAIN:], preferred_element_type=F32)
        for p in range(3):
            if first == 0:
                tok_loads[p].wait()
            main = jnp.dot(pick, tok[:, p * PART:(p + 1) * PART], preferred_element_type=F32)
            tail = tails[p * 8 * count:(p + 1) * 8 * count].reshape(count, 8, PART)
            both = jnp.concatenate([tail, tail], axis=1)
            block = jnp.where(tail_mask, both, main.reshape(count, 16, PART)).astype(BF16)
            send[first:first + count, :, p * PART:(p + 1) * PART] = block

    for first, count in CHUNKS:
        build(first, count)
        if first == 0:
            pl.semaphore_wait(barrier, N_EXP)
            self_rows.start()
            self_prob.start()

        for i in range(max(first, 1), min(first + count, 8 * AHEAD)):
            send_copy(i // 8, i % 2, ((i % 8) // 2 + 2 * (i % 2)) % 4).start()
            prob_copy(i // 8, i % 2, ((i % 8) // 2 + 2 * (i % 2)) % 4).start()

    for load in w_loads:
        load.wait()

    def forward_copy(k):
        return pltpu.make_async_remote_copy(
            rows.at[k, g], rows.at[k, g], fwds_sem.at[k], fwdr_sem.at[k], device_id=partner, device_id_type=MESH)

    def prob_forward(k):
        part = pl.ds(k * 8, 8)
        return pltpu.make_async_remote_copy(
            pr_own.at[part], pr_part.at[part], pfs_sem.at[k], pfr_sem.at[k], device_id=partner, device_id_type=MESH)

    low = lax.broadcasted_iota(I32, (8, PART), 0) < 4

    def unpack(k, m):
        base = (k * 2 + m) * 4

        def half(s, h, p):
            return recv[base + s, :, p * PART:(p + 1) * PART].astype(F32)[8 * h:8 * h + 8]

        def put(t, p, lo, hi):
            rows[k, g, m * GROUP + 16 * t:m * GROUP + 16 * t + 16, p * PART:(p + 1) * PART] = jnp.concatenate(
                [lo, hi], axis=0).astype(BF16)

        for p in range(3):
            put(0, p, half(0, 0, p), jnp.where(low, half(0, 1, p), half(1, 1, p)))
            put(1, p, half(1, 0, p), half(2, 1, p))
            put(2, p, jnp.where(low, half(2, 0, p), half(3, 0, p)), half(3, 1, p))

        def quad(q):
            s, p = q // 3, q % 3
            at = 3 - s
            value = half(s, at // 2, p)
            return value if at % 2 == q % 2 else pltpu.roll(value, 4, 0)

        for t in range(3):
            lo, hi = (jnp.where(low, quad(4 * t + 2 * h), quad(4 * t + 2 * h + 1)) for h in range(2))
            put(t, 3, lo, hi)

    row16 = lax.broadcasted_iota(I32, (ROWS, 16), 0)
    at16 = lax.broadcasted_iota(I32, (ROWS, 16), 1) * CAP
    spread = jnp.where((row16 >= at16) & (row16 < at16 + CAP), 1.0, 0.0)
    row_t = lax.broadcasted_iota(I32, (16, ROWS), 1)
    at_t = lax.broadcasted_iota(I32, (16, ROWS), 0) * CAP
    spread_t = jnp.where((row_t >= at_t) & (row_t < at_t + CAP), 1.0, 0.0)
    row128 = lax.broadcasted_iota(I32, (ROWS, 128), 0)
    lane_hit = lax.broadcasted_iota(I32, (ROWS, 128), 1) == row128 - ((row128 * 5462) >> 16) * CAP

    def product(k, count, sl):
        left = rows[pl.ds(k, count), :, :, sl].reshape(count * ROWS, TILE)
        right = terms[pl.ds(k, count)].reshape(count * ROWS, 2 * HALF)
        return lax.dot_general(left, right, (((0,), (0,)), ((), ())), preferred_element_type=F32)

    def tile(i):
        return pl.ds(pl.multiple_of(i * TILE, TILE), TILE)

    def put_grads(i, value, add):
        for ref, half in ((gg_ref, value[:, :HALF]), (gu_ref, value[:, HALF:])):
            if add:
                half = half + ref[0, tile(i), :].astype(F32)
            ref[0, tile(i), :] = half.astype(BF16)

    def accumulate(k):
        odd = lax.rem(k, 2)
        first_tile, last_tile = 2 * odd, 2 + 2 * odd

        @pl.when((k == 4) | (k == 5))
        def _():
            @pl.loop(first_tile, last_tile)
            def _(i):
                put_grads(i, product(0, 4, tile(i)), False)

        @pl.when(k >= 6)
        def _():
            @pl.loop(first_tile, last_tile)
            def _(i):
                put_grads(i, product(4, 2, tile(i)), True)

    def step(k):
        first = k == 0

        @pl.when(first)
        def _():
            peers_copy(send, recv, 0, send_sem, recv_sem.at[0], 3).wait_recv()
            peers_copy(prs, pr_own, 0, prs_sem, prr_sem.at[0], 7).wait_recv()
            self_rows.wait()
            self_prob.wait()

        @pl.when(jnp.logical_not(first))
        def _():
            peers_copy(send, recv, 0, send_sem, recv_sem.at[2 * k], 4).wait_recv()
            peers_copy(prs, pr_own, 0, prs_sem, prr_sem.at[k], 8).wait_recv()

        peers_copy(send, recv, 0, send_sem, recv_sem.at[2 * k + 1], 4).wait_recv()

        @pl.when(k < STEPS - AHEAD)
        def _():
            send_step(k + AHEAD)

        groups = [group_of(k, 0), group_of(k, 1)]
        prob_forward(k).start()
        unpack(k, 0)
        unpack(k, 1)
        forward = forward_copy(k)
        forward.start()

        accumulate(k)

        prob_forward(k).wait_recv()
        own_p, other_p = pr_own[pl.ds(k * 8, 8), 0, :], pr_part[pl.ds(k * 8, 8), 0, :]
        mine = g == 0
        probs = jnp.concatenate([jnp.where(mine, own_p, other_p), jnp.where(mine, other_p, own_p)], axis=0)
        probs = jnp.dot(spread.astype(BF16), probs.astype(BF16), preferred_element_type=F32)
        prob = jnp.sum(jnp.where(lane_hit, probs, 0.0), axis=1, keepdims=True)
        forward.wait_recv()

        total = jnp.zeros((ROWS, 1), F32)
        width = 256
        for n in range(HALF // width):
            sl = slice(n * width, (n + 1) * width)
            here = rows[k].reshape(ROWS, D)
            gate = jnp.dot(here, wg[:, sl], preferred_element_type=F32)
            up = jnp.dot(here, wu[:, sl], preferred_element_type=F32)
            pieces = [
                hg[pl.ds(pl.multiple_of(j * 768 + groups[m] * GROUP, 16), GROUP), sl] for j in range(2) for m in range(2)]
            cot = jnp.concatenate(pieces, axis=0).astype(F32)
            sig = jax.nn.sigmoid(gate)
            act = gate * sig
            total = total + jnp.sum(act * up * cot, axis=1, keepdims=True)
            scaled = prob * cot
            terms[k, :, sl] = (scaled * up * sig * (1.0 + gate * (1.0 - sig))).astype(BF16)
            terms[k, :, HALF + n * width:HALF + (n + 1) * width] = (scaled * act).astype(BF16)
        by_source = jnp.dot(
            spread_t, jnp.where(lane_hit, total, 0.0), precision=HIGH, preferred_element_type=F32)
        for j in range(2):
            ret_out[pl.ds(j * N_EXP + k * 8, 8), 0, :] = by_source[8 * j:8 * j + 8]
        for m in range(2):
            for s in range(4):
                for j in range(2):
                    copy = return_copy(k, m, s, groups[m], j)
                    if m == 0:
                        own = (k == 0) & (x == s) & (g == j)
                        pl.when(own)(self_ret.start)
                        pl.when(jnp.logical_not(own))(copy.start)
                    else:
                        copy.start()

    @pl.loop(0, STEPS)
    def _(k):
        step(k)

    @pl.loop(0, D // TILE)
    def _(i):
        put_grads(i, product(STEPS - 2, 2, tile(i)), True)

    peers_copy(ret_out, ret_own, 0, rets_sem, retr_sem, 2 * N_EXP - 1).wait_recv()
    self_ret.wait()
    sums = ret_own[0:N_EXP, 0, :] + ret_own[N_EXP:, 0, :]
    by_slot = lax.dot_general(
        sums, member_ref[...], (((0,), (0,)), ((), ())), precision=HIGH, preferred_element_type=F32)
    pg_ref[...] = jnp.sum(jnp.where(lane_slot == pos, by_slot, 0.0), axis=0, keepdims=True)

    peers_copy(send, recv, 0, send_sem, recv_sem.at[0]).wait_send()
    peers_copy(prs, pr_own, 0, prs_sem, prr_sem.at[0]).wait_send()
    peers_copy(ret_out, ret_own, 0, rets_sem, retr_sem, 2 * N_EXP - 1).wait_send()

    @pl.loop(0, STEPS)
    def _(k):
        forward_copy(k).wait_send()
        prob_forward(k).wait_send()


def body(tokens, routes, gate_prob, w_gate, w_up, hidden_grad):
    hbm = pl.BlockSpec(memory_space=pl.ANY)
    vmem = pl.BlockSpec(memory_space=pltpu.VMEM)
    dma = pltpu.SemaphoreType.DMA
    grad = pltpu.VMEM((1, D, HALF), BF16)
    grad_gate, grad_up, prob_grad = pl.pallas_call(
        kernel,
        out_shape=(grad, grad, jax.ShapeDtypeStruct((1, TOK), F32)),
        in_specs=[hbm, vmem, vmem, hbm, hbm, hbm],
        out_specs=(vmem, vmem, vmem),
        scratch_shapes=[
            pltpu.VMEM((TOK, D), BF16),
            pltpu.VMEM((N_EXP, 16, MAIN), BF16),
            pltpu.VMEM((N_EXP, 16, MAIN), BF16),
            pltpu.VMEM((STEPS, 2, 2 * GROUP, D), BF16),
            pltpu.VMEM((D, HALF), BF16),
            pltpu.VMEM((D, HALF), BF16),
            pltpu.VMEM((1536, HALF), BF16),
            pltpu.VMEM((STEPS, ROWS, 2 * HALF), BF16),
            pltpu.VMEM((N_EXP, TOK), F32),
            pltpu.VMEM((N_EXP, 1, 128), F32),
            pltpu.VMEM((N_EXP, 1, 128), F32),
            pltpu.VMEM((N_EXP, 1, 128), F32),
            pltpu.VMEM((2 * N_EXP, 1, 128), F32),
            pltpu.VMEM((2 * N_EXP, 1, 128), F32),
            dma, dma((2 * STEPS,)), dma, dma((STEPS,)), dma, dma,
            dma((STEPS,)), dma((STEPS,)), dma((STEPS,)), dma((STEPS,)), dma((7,)), dma((3,)),
        ],
        compiler_params=pltpu.CompilerParams(
            collective_id=0, has_side_effects=True, vmem_limit_bytes=54 * 1024 * 1024),
        cost_estimate=pl.CostEstimate(flops=26 * 10**9, bytes_accessed=20 * 10**6, transcendentals=10**6),
        name="moe_grads",
    )(tokens, routes.reshape(1, TOK), gate_prob.reshape(1, TOK), w_gate, w_up, hidden_grad)
    return grad_gate, grad_up, prob_grad.reshape(TOK, 1)


def solution(mesh):
    in_specs = (
        P(("exp", "grp"), None),
        P(("exp", "grp"), None),
        P(("exp", "grp"), None),
        P("exp", None, "grp"),
        P("exp", None, "grp"),
        P("exp", None, "grp"),
    )
    out_specs = (P("exp", None, "grp"), P("exp", None, "grp"), P(("exp", "grp"), None))
    return jax.shard_map(body, mesh=mesh, in_specs=in_specs, out_specs=out_specs, check_vma=False)
```
